32 devices in a mesh: groups: 2 (over y), blk: 4 (over z), panel: 4 (over x, core).
Axes of the slice: x: 2, y: 2, z: 4, core: 2. Of those that a mesh axis runs over, the one named last changes fastest.
Arguments:
- points: bfloat16 [4096, 256], P(('groups', 'blk', 'panel')), parts along dimension 0, may hold values from -6 to 6
- targets: float32 [4096, 64], P(('groups', 'blk', 'panel')), parts along dimension 0, may hold values from -6 to 6
Outputs:
- solution: float32 [4096, 64], P(('groups', 'blk', 'panel')), parts along dimension 0
- residual: float32 [4096, 64], P(('groups', 'blk', 'panel')), parts along dimension 0
- direction: float32 [4096, 64], P(('groups', 'blk', 'panel')), parts along dimension 0
The draws below stay inside these ranges and needn't reach their ends.
There are 2 independent parts, one for each index of `groups`. The reference program is written for one: setup_inputs(seed, part) draws one part's arguments, and reference() takes and returns one part's arrays. A program takes and returns all parts, laid end to end along the dimension named above; each array names one. Nothing has to cross between parts.
All inputs are finite; a program needn't handle non-finite values.
Results may differ from the reference program's by a relative error of at most 0.001.
The reference program's roundings to bfloat16 on the way count: a program that leaves them out, or rounds other values in their place, can miss the bound.
Values may be sent and summed in bfloat16 or wider, within the bound.
A program may use at most 64 MiB of HBM per device.

```python
import jax
import jax.numpy as jnp
from jax import lax

D = 256
COLS = 64
POINTS = 2048


def draw_targets(key, part):
    key = jax.random.fold_in(key, 7)
    key_point, key_sign, key_noise = jax.random.split(key, 3)
    column_signs = (2 * jax.random.randint(key_sign, (1, COLS), 0, 2) - 1).astype(jnp.float32)
    shared = jax.random.normal(key_point, (POINTS, 1), jnp.float32)
    independent = 0.3 * jax.random.normal(key_noise, (POINTS, COLS), jnp.float32)
    values = 2.0 * shared * column_signs + independent
    return jnp.clip(values, -6.0, 6.0)


def shard_levels(stream_key, shape, shards, smallest, high):
    gain, own = 1.0, jax.random.fold_in(stream_key, 6)
    for position, parts in shards:
        heights = jnp.exp(jax.random.uniform(jax.random.fold_in(own, position), (parts,), jnp.float32, smallest / len(shards), high / len(shards)))
        gain = gain * jnp.repeat(heights, shape[position] // parts).reshape([-1 if axis == position else 1 for axis in range(len(shape))])
    return gain


def scatter_about(own_key, extent, spread, limit, cuts=(), held_as=jnp.bfloat16):
    result = spread * jax.random.normal(own_key, extent, jnp.float32)
    if cuts:
        result = result * shard_levels(own_key, extent, cuts, -0.22, 0.18)
    return jnp.clip(result, -limit, limit).astype(held_as)


def setup_inputs(seed: int = 0, part: int = 0) -> dict:
    splits = jax.random.split(jax.random.key(seed), 3)
    part_keys = jax.random.split(jax.random.fold_in(splits[2], part), 3)
    points = scatter_about(part_keys[0], (POINTS, D), 1.0, 6.0, ((0, 16),))
    targets = draw_targets(jax.random.fold_in(jax.random.fold_in(splits[2], part), 71), part)
    return dict(points=points, targets=targets)


def kernel_tile(query, sq_query, keys, sq_keys, ell2):
    cross = jnp.einsum('qd,kd->qk', query.astype(jnp.float32), keys.astype(jnp.float32), preferred_element_type=jnp.float32)
    dist = jnp.maximum(sq_query[:, None] + sq_keys[None, :] - 2.0 * cross, 0.0)
    return jnp.exp(-dist / (2.0 * ell2)).astype(jnp.bfloat16)

def reference(points, targets):
    highest = lax.Precision.HIGHEST
    ell2 = D / 4.0
    wide = points.astype(jnp.float32)
    sqnorm = jnp.sum(wide * wide, axis=1)
    dir_low = targets.astype(jnp.bfloat16)
    block_rows = 512 if POINTS % 512 == 0 else POINTS
    count = POINTS // block_rows
    query_blocks = points.reshape(count, block_rows, D)
    sq_blocks = sqnorm.reshape(count, block_rows)

    def one_block(pair):
        tile = kernel_tile(pair[0], pair[1], points, sqnorm, ell2)
        return jnp.dot(tile.astype(jnp.float32), dir_low.astype(jnp.float32), preferred_element_type=jnp.float32)
    products = lax.map(one_block, (query_blocks, sq_blocks)).reshape(POINTS, COLS)
    image = 1.0 * targets + products
    gram = jnp.dot(targets.T, targets, precision=highest)
    curv = jnp.dot(targets.T, image, precision=highest)
    alpha = jax.scipy.linalg.cho_solve((jnp.linalg.cholesky(curv), True), gram)
    solution = jnp.dot(targets, alpha, precision=highest)
    residual = targets - jnp.dot(image, alpha, precision=highest)
    newgram = jnp.dot(residual.T, residual, precision=highest)
    beta = jax.scipy.linalg.cho_solve((jnp.linalg.cholesky(gram), True), newgram)
    direction = residual + jnp.dot(targets, beta, precision=highest)
    return (solution, residual, direction)
```

```python
import functools

import jax
import jax.numpy as jnp
from jax import lax
from jax.experimental import pallas as pl
from jax.experimental.pallas import tpu as pltpu
from jax.sharding import PartitionSpec as P

MESH = pl.DeviceIdType.MESH
HIGHEST = lax.Precision.HIGHEST
STEP = 8


def each(count, body):
    if count <= 8:
        for offset in range(1, count):
            body(offset)
    else:
        lax.fori_loop(1, count, lambda offset, carry: (body(offset), carry)[1], 0)


def dot_nt(a, b, precision=None):
    return lax.dot_general(
        a, b, (((1,), (1,)), ((), ())), precision=precision, preferred_element_type=jnp.float32
    )


def dot(a, b, precision=HIGHEST):
    return jnp.dot(a, b, precision=precision, preferred_element_type=jnp.float32)


def eliminate(whole, rows):
    width = whole.shape[1]
    blocks = [whole[i : i + STEP, :] for i in range(0, rows, STEP)]
    sub = lax.broadcasted_iota(jnp.int32, (STEP, width), 0)
    for k in range(rows // STEP):
        lead = blocks[k]
        spread = [
            [
                jnp.broadcast_to(block[:, k * STEP + j : k * STEP + j + 1], (STEP, width))
                for j in range(STEP)
            ]
            for block in blocks
        ]
        cols = list(spread[k])
        scales = jnp.ones((STEP, width), jnp.float32)
        for j in range(STEP):
            inverse = 1.0 / jnp.broadcast_to(cols[j][j : j + 1, :], (STEP, width))
            factor = jnp.where(sub == j, 0.0, cols[j] * inverse)
            scales = jnp.where(sub == j, inverse, scales)
            lead = lead - factor * jnp.broadcast_to(lead[j : j + 1, :], (STEP, width))
            for i in range(j + 1, STEP):
                cols[i] = cols[i] - factor * jnp.broadcast_to(cols[i][j : j + 1, :], (STEP, width))
        lead = lead * scales
        lead_rows = [jnp.broadcast_to(lead[j : j + 1, :], (STEP, width)) for j in range(STEP)]
        for i in range(rows // STEP):
            if i == k:
                blocks[i] = lead
            else:
                total = spread[i][0] * lead_rows[0]
                for j in range(1, STEP):
                    total = total + spread[i][j] * lead_rows[j]
                blocks[i] = blocks[i] - total
    return jnp.concatenate(blocks, axis=0)


def kernel(
    panels,
    blks,
    points_ref,
    targets_ref,
    solution_ref,
    residual_ref,
    direction_ref,
    queries,
    keys,
    dirs,
    parts,
    part_in,
    gram_own,
    gram_part,
    gram_chunk,
    gram_sum,
    small_own,
    small_part,
    small_chunk,
    small_sum,
    gram_inv,
    query_sems,
    key_sems,
    dir_sems,
    part_sems,
    gram_sems_part,
    gram_sems_chunk,
    gram_sems_sum,
    small_sems_part,
    small_sems_chunk,
    small_sems_sum,
):
    rows, depth = points_ref.shape
    wide_cols = targets_ref.shape[1]
    my_panel = lax.axis_index("panel")
    my_blk = lax.axis_index("blk")
    scale = 2.0 / depth

    def panel_at(offset):
        return {"panel": lax.rem(my_panel + offset, panels)}

    def blk_at(offset):
        return {"blk": lax.rem(my_blk + offset, blks)}

    def send(source, target, sems, index, device):
        return pltpu.make_async_remote_copy(
            src_ref=source,
            dst_ref=target,
            send_sem=sems.at[0, index],
            recv_sem=sems.at[1, index],
            device_id=device,
            device_id_type=MESH,
        )

    barrier = pltpu.get_barrier_semaphore()
    each(panels, lambda d: pl.semaphore_signal(barrier, inc=1, device_id=panel_at(d), device_id_type=MESH))
    each(blks, lambda d: pl.semaphore_signal(barrier, inc=1, device_id=blk_at(d), device_id_type=MESH))

    targets = targets_ref[...]
    targets_t = targets.T
    keys[0] = points_ref[...]
    queries[0] = points_ref[...]
    dirs[0] = targets_t.astype(jnp.bfloat16)
    double = jnp.concatenate([targets_t, targets_t], axis=0)
    gram_own[...] = dot_nt(targets_t, double, HIGHEST)
    pl.semaphore_wait(barrier, panels - 1 + blks - 1)

    def copy_query(d):
        return send(queries.at[0], queries.at[d], query_sems, d, panel_at(d))

    def copy_key(d):
        return send(keys.at[0], keys.at[d], key_sems, d, blk_at(d))

    def copy_dir(d):
        return send(dirs.at[0], dirs.at[d], dir_sems, d, blk_at(d))

    chunk = wide_cols // panels
    my_rows = pl.ds(pl.multiple_of(my_panel * chunk, 8), chunk)

    def scatter_copy(own, part, sems, d):
        owner = lax.rem(my_panel + d, panels)
        there = pl.ds(pl.multiple_of(owner * chunk, 8), chunk)
        return send(own.at[there, :], part.at[d], sems, d, panel_at(d))

    def scatter_start(own, part, sems):
        each(panels, lambda d: scatter_copy(own, part, sems, d).start())

    def exchange_copy(chunks, sems, d):
        return send(chunks.at[0], chunks.at[d], sems, d, blk_at(d))

    def exchange_start(own, part, sems, chunks, chunk_sems):
        each(panels, lambda d: scatter_copy(own, part, sems, d).wait())
        part[0] = own[my_rows, :]
        chunks[0] = jnp.sum(part[...], axis=0)
        each(blks, lambda d: exchange_copy(chunks, chunk_sems, d).start())

    def gather_copy(result, sems, d):
        return send(result.at[my_rows, :], result.at[my_rows, :], sems, d, panel_at(d))

    def gather_start(chunks, chunk_sems, result, sems):
        each(blks, lambda d: exchange_copy(chunks, chunk_sems, d).wait())
        result[my_rows, :] = jnp.sum(chunks[...], axis=0)
        each(panels, lambda d: gather_copy(result, sems, d).start())

    def gather_wait(result, sems):
        def one(d):
            back = lax.rem(my_panel + panels - d, panels)
            there = pl.ds(pl.multiple_of(back * chunk, 8), chunk)
            gather_copy(result, sems, d).wait_send()
            send(result.at[there, :], result.at[there, :], sems, d, panel_at(d)).wait_recv()

        each(panels, one)

    scatter_start(gram_own, gram_part, gram_sems_part)
    each(blks, lambda d: copy_key(d).start())
    each(blks, lambda d: copy_dir(d).start())
    each(panels, lambda d: copy_query(d).start())

    exchange_start(gram_own, gram_part, gram_sems_part, gram_chunk, gram_sems_chunk)
    gather_start(gram_chunk, gram_sems_chunk, gram_sum, gram_sems_sum)

    each(panels, lambda d: copy_query(d).wait())
    all_queries = queries[...].reshape(panels * rows, depth)
    wide = all_queries.astype(jnp.float32)
    sq_queries = dot_nt(jnp.full((8, depth), scale, jnp.float32), wide * wide, HIGHEST)[0:1, :]

    def tile(d):
        key = keys[d]
        wide_key = key.astype(jnp.float32)
        sq_key = jnp.sum(wide_key * wide_key, axis=1, keepdims=True) * scale
        cross = dot_nt(key, all_queries)
        weight = jnp.exp(jnp.minimum((2.0 * scale) * cross - sq_key - sq_queries, 0.0)).astype(jnp.bfloat16)
        return jnp.dot(dirs[d], weight, preferred_element_type=jnp.float32)

    first = tile(0)
    for p in range(panels):
        parts[p] = first[:, p * rows : (p + 1) * rows]

    gather_wait(gram_sum, gram_sems_sum)
    lane = lax.broadcasted_iota(jnp.int32, (wide_cols, 2 * wide_cols), 1)
    line = lax.broadcasted_iota(jnp.int32, (wide_cols, 2 * wide_cols), 0)
    gram2 = gram_sum[...]
    unit = (lane == line + wide_cols).astype(jnp.float32)
    gram_inv[...] = eliminate(jnp.where(lane < wide_cols, gram2, unit), wide_cols)

    def more(d):
        copy_key(d).wait()
        copy_dir(d).wait()
        value = tile(d)
        for p in range(panels):
            parts[p] += value[:, p * rows : (p + 1) * rows]

    each(blks, more)

    def copy_part(d):
        return send(parts.at[d], part_in.at[d], part_sems, d, panel_at(panels - d))

    each(panels, lambda d: copy_part(d).start())
    each(panels, lambda d: copy_part(d).wait())
    part_in[0] = parts[0]
    image_t = 1.0 * targets_t + jnp.sum(part_in[...], axis=0)
    small_own[...] = dot_nt(image_t, jnp.concatenate([targets_t, image_t], axis=0), HIGHEST)
    scatter_start(small_own, small_part, small_sems_part)
    both = jnp.concatenate([targets, image_t.T], axis=0)
    exchange_start(small_own, small_part, small_sems_part, small_chunk, small_sems_chunk)
    gather_start(small_chunk, small_sems_chunk, small_sum, small_sems_sum)
    gather_wait(small_sum, small_sems_sum)

    small = small_sum[...]
    curv_t = small[:, :wide_cols]
    quad = small[:, wide_cols:]
    curv = curv_t.T
    symmetric = 0.5 * (curv + curv_t)
    start = jnp.where(lane < wide_cols, jnp.concatenate([symmetric, symmetric], axis=1), gram2)
    alpha = eliminate(start, wide_cols)[:, wide_cols:]
    gram = gram2[:, :wide_cols]
    inner = dot(jnp.concatenate([quad, curv], axis=0), alpha)
    newgram = gram - inner[wide_cols:] + dot(alpha.T, inner[:wide_cols] - curv_t)
    made = dot(both, alpha)
    residual = targets - made[rows:]
    solution_ref[...] = made[:rows]
    residual_ref[...] = residual
    beta = dot(gram_inv[:, wide_cols:], newgram)
    direction_ref[...] = residual + dot(targets, beta)


def solution(mesh):
    panels, blks = mesh.shape["panel"], mesh.shape["blk"]

    def local(points, targets):
        rows, depth = points.shape
        cols = targets.shape[1]
        chunk = cols // panels
        f32, bf16 = jnp.float32, jnp.bfloat16
        out = jax.ShapeDtypeStruct((rows, cols), f32)
        vmem = pl.BlockSpec(memory_space=pltpu.VMEM)
        small = [
            pltpu.VMEM((cols, 2 * cols), f32),
            pltpu.VMEM((panels, chunk, 2 * cols), f32),
            pltpu.VMEM((blks, chunk, 2 * cols), f32),
            pltpu.VMEM((cols, 2 * cols), f32),
        ]
        panel_sems = pltpu.SemaphoreType.DMA((2, panels))
        blk_sems = pltpu.SemaphoreType.DMA((2, blks))
        return pl.pallas_call(
            functools.partial(kernel, panels, blks),
            out_shape=(out, out, out),
            in_specs=[vmem, vmem],
            out_specs=(vmem, vmem, vmem),
            scratch_shapes=[
                pltpu.VMEM((panels, rows, depth), bf16),
                pltpu.VMEM((blks, rows, depth), bf16),
                pltpu.VMEM((blks, cols, rows), bf16),
                pltpu.VMEM((panels, cols, rows), f32),
                pltpu.VMEM((panels, cols, rows), f32),
                *small,
                *small,
                pltpu.VMEM((cols, 2 * cols), f32),
                panel_sems,
                blk_sems,
                blk_sems,
                panel_sems,
                panel_sems,
                blk_sems,
                panel_sems,
                panel_sems,
                blk_sems,
                panel_sems,
            ],
            compiler_params=pltpu.CompilerParams(
                collective_id=0, has_side_effects=True, vmem_limit_bytes=48 * 1024 * 1024
            ),
        )(points, targets)

    placed = P(("groups", "blk", "panel"), None)
    return jax.shard_map(
        local,
        mesh=mesh,
        in_specs=(placed, placed),
        out_specs=(placed, placed, placed),
        check_vma=False,
    )
```

```python
import functools

import jax
import jax.numpy as jnp
from jax import lax
from jax.experimental import pallas as pl
from jax.experimental.pallas import tpu as pltpu
from jax.sharding import PartitionSpec as P

MESH = pl.DeviceIdType.MESH
HIGHEST = lax.Precision.HIGHEST
STEP = 8


def each(count, body):
    if count <= 8:
        for offset in range(1, count):
            body(offset)
    else:
        lax.fori_loop(1, count, lambda offset, carry: (body(offset), carry)[1], 0)


def dot_nt(a, b, precision=None):
    return lax.dot_general(
        a, b, (((1,), (1,)), ((), ())), precision=precision, preferred_element_type=jnp.float32
    )


def dot(a, b, precision=HIGHEST):
    return jnp.dot(a, b, precision=precision, preferred_element_type=jnp.float32)


def eliminate(whole, rows):
    width = whole.shape[1]
    blocks = [whole[i : i + STEP, :] for i in range(0, rows, STEP)]
    sub = lax.broadcasted_iota(jnp.int32, (STEP, width), 0)
    for k in range(rows // STEP):
        lead = blocks[k]
        spread = [
            [
                jnp.broadcast_to(block[:, k * STEP + j : k * STEP + j + 1], (STEP, width))
                for j in range(STEP)
            ]
            for block in blocks
        ]
        cols = list(spread[k])
        scales = jnp.ones((STEP, width), jnp.float32)
        for j in range(STEP):
            inverse = 1.0 / jnp.broadcast_to(cols[j][j : j + 1, :], (STEP, width))
            factor = jnp.where(sub == j, 0.0, cols[j] * inverse)
            scales = jnp.where(sub == j, inverse, scales)
            lead = lead - factor * jnp.broadcast_to(lead[j : j + 1, :], (STEP, width))
            for i in range(j + 1, STEP):
                cols[i] = cols[i] - factor * jnp.broadcast_to(cols[i][j : j + 1, :], (STEP, width))
        lead = lead * scales
        lead_rows = [jnp.broadcast_to(lead[j : j + 1, :], (STEP, width)) for j in range(STEP)]
        for i in range(rows // STEP):
            if i == k:
                blocks[i] = lead
            else:
                total = spread[i][0] * lead_rows[0]
                for j in range(1, STEP):
                    total = total + spread[i][j] * lead_rows[j]
                blocks[i] = blocks[i] - total
    return jnp.concatenate(blocks, axis=0)


def kernel(
    panels,
    blks,
    points_ref,
    targets_ref,
    solution_ref,
    residual_ref,
    direction_ref,
    queries,
    keys,
    dirs,
    parts,
    part_in,
    gram_own,
    gram_part,
    gram_chunk,
    gram_sum,
    small_own,
    small_part,
    small_chunk,
    small_sum,
    solved,
    query_sems,
    key_sems,
    dir_sems,
    part_sems,
    gram_sems_part,
    gram_sems_chunk,
    gram_sems_sum,
    small_sems_part,
    small_sems_chunk,
    small_sems_sum,
):
    rows, depth = points_ref.shape
    wide_cols = targets_ref.shape[0]
    my_panel = lax.axis_index("panel")
    my_blk = lax.axis_index("blk")
    scale = 2.0 / depth

    def panel_at(offset):
        return {"panel": lax.rem(my_panel + offset, panels)}

    def blk_at(offset):
        return {"blk": lax.rem(my_blk + offset, blks)}

    def send(source, target, sems, index, device):
        return pltpu.make_async_remote_copy(
            src_ref=source,
            dst_ref=target,
            send_sem=sems.at[0, index],
            recv_sem=sems.at[1, index],
            device_id=device,
            device_id_type=MESH,
        )

    barrier = pltpu.get_barrier_semaphore()
    each(panels, lambda d: pl.semaphore_signal(barrier, inc=1, device_id=panel_at(d), device_id_type=MESH))
    each(blks, lambda d: pl.semaphore_signal(barrier, inc=1, device_id=blk_at(d), device_id_type=MESH))

    targets_t = targets_ref[...]
    keys[0] = points_ref[...]
    queries[0] = points_ref[...]
    dirs[0] = targets_t.astype(jnp.bfloat16)
    double = jnp.concatenate([targets_t, targets_t], axis=0)
    gram_own[...] = dot_nt(targets_t, double, HIGHEST)
    pl.semaphore_wait(barrier, panels - 1 + blks - 1)

    def copy_query(d):
        return send(queries.at[0], queries.at[d], query_sems, d, panel_at(d))

    def copy_key(d):
        return send(keys.at[0], keys.at[d], key_sems, d, blk_at(d))

    def copy_dir(d):
        return send(dirs.at[0], dirs.at[d], dir_sems, d, blk_at(d))

    chunk = wide_cols // panels
    my_rows = pl.ds(pl.multiple_of(my_panel * chunk, 8), chunk)

    def scatter_copy(own, part, sems, d):
        owner = lax.rem(my_panel + d, panels)
        there = pl.ds(pl.multiple_of(owner * chunk, 8), chunk)
        return send(own.at[there, :], part.at[d], sems, d, panel_at(d))

    def scatter_start(own, part, sems):
        each(panels, lambda d: scatter_copy(own, part, sems, d).start())

    def exchange_copy(chunks, sems, d):
        return send(chunks.at[0], chunks.at[d], sems, d, blk_at(d))

    def exchange_start(own, part, sems, chunks, chunk_sems):
        each(panels, lambda d: scatter_copy(own, part, sems, d).wait())
        part[0] = own[my_rows, :]
        chunks[0] = jnp.sum(part[...], axis=0)
        each(blks, lambda d: exchange_copy(chunks, chunk_sems, d).start())

    def gather_copy(result, sems, d):
        return send(result.at[my_rows, :], result.at[my_rows, :], sems, d, panel_at(d))

    def gather_start(chunks, chunk_sems, result, sems):
        each(blks, lambda d: exchange_copy(chunks, chunk_sems, d).wait())
        result[my_rows, :] = jnp.sum(chunks[...], axis=0)
        each(panels, lambda d: gather_copy(result, sems, d).start())

    def gather_wait(result, sems):
        def one(d):
            back = lax.rem(my_panel + panels - d, panels)
            there = pl.ds(pl.multiple_of(back * chunk, 8), chunk)
            gather_copy(result, sems, d).wait_send()
            send(result.at[there, :], result.at[there, :], sems, d, panel_at(d)).wait_recv()

        each(panels, one)

    scatter_start(gram_own, gram_part, gram_sems_part)
    each(blks, lambda d: copy_key(d).start())
    each(blks, lambda d: copy_dir(d).start())
    each(panels, lambda d: copy_query(d).start())

    exchange_start(gram_own, gram_part, gram_sems_part, gram_chunk, gram_sems_chunk)
    gather_start(gram_chunk, gram_sems_chunk, gram_sum, gram_sems_sum)

    each(panels, lambda d: copy_query(d).wait())
    all_queries = queries[...].reshape(panels * rows, depth)
    wide = all_queries.astype(jnp.float32)
    sq_queries = dot_nt(jnp.full((8, depth), scale, jnp.float32), wide * wide, HIGHEST)[0:1, :]

    def tile(d):
        key = keys[d]
        wide_key = key.astype(jnp.float32)
        sq_key = jnp.sum(wide_key * wide_key, axis=1, keepdims=True) * scale
        cross = dot_nt(key, all_queries)
        weight = jnp.exp(jnp.minimum((2.0 * scale) * cross - sq_key - sq_queries, 0.0)).astype(jnp.bfloat16)
        return jnp.dot(dirs[d], weight, preferred_element_type=jnp.float32)

    first = tile(0)
    for p in range(panels):
        parts[p] = first[:, p * rows : (p + 1) * rows]

    def more(d):
        copy_key(d).wait()
        copy_dir(d).wait()
        value = tile(d)
        for p in range(panels):
            parts[p] += value[:, p * rows : (p + 1) * rows]

    each(blks, more)

    def copy_part(d):
        return send(parts.at[d], part_in.at[d], part_sems, d, panel_at(panels - d))

    each(panels, lambda d: copy_part(d).start())
    gather_wait(gram_sum, gram_sems_sum)
    lane = lax.broadcasted_iota(jnp.int32, (wide_cols, 2 * wide_cols), 1)
    line = lax.broadcasted_iota(jnp.int32, (wide_cols, 2 * wide_cols), 0)
    gram2 = gram_sum[...]
    unit = (lane == line + wide_cols).astype(jnp.float32)
    gram_inv = eliminate(jnp.where(lane < wide_cols, gram2, unit), wide_cols)[:, wide_cols:]
    solved[...] = dot(gram_inv, targets_t)

    each(panels, lambda d: copy_part(d).wait())
    part_in[0] = parts[0]
    image_t = 1.0 * targets_t + jnp.sum(part_in[...], axis=0)
    small_own[...] = dot_nt(image_t, jnp.concatenate([targets_t, image_t], axis=0), HIGHEST)
    scatter_start(small_own, small_part, small_sems_part)
    both = jnp.concatenate([targets_t, image_t], axis=1)
    exchange_start(small_own, small_part, small_sems_part, small_chunk, small_sems_chunk)
    gather_start(small_chunk, small_sems_chunk, small_sum, small_sems_sum)
    gather_wait(small_sum, small_sems_sum)

    small = small_sum[...]
    curv_t = small[:, :wide_cols]
    curv = curv_t.T
    symmetric = 0.5 * (curv + curv_t)
    start = jnp.where(lane < wide_cols, jnp.concatenate([symmetric, symmetric], axis=1), gram2)
    alpha_t = eliminate(start, wide_cols)[:, wide_cols:].T
    gram = gram2[:, :wide_cols]
    made = dot(alpha_t, both)
    residual = targets_t - made[:, rows:]
    solution_ref[...] = made[:, :rows]
    residual_ref[...] = residual
    inner = dot(alpha_t, small)
    newgram = gram - inner[:, :wide_cols] + dot_nt(inner[:, wide_cols:] - curv, alpha_t, HIGHEST)
    direction_ref[...] = residual + dot(newgram, solved[...])


def solution(mesh):
    panels, blks = mesh.shape["panel"], mesh.shape["blk"]

    def local(points, targets):
        rows, depth = points.shape
        cols = targets.shape[1]
        chunk = cols // panels
        f32, bf16 = jnp.float32, jnp.bfloat16
        out = jax.ShapeDtypeStruct((cols, rows), f32)
        vmem = pl.BlockSpec(memory_space=pltpu.VMEM)
        small = [
            pltpu.VMEM((cols, 2 * cols), f32),
            pltpu.VMEM((panels, chunk, 2 * cols), f32),
            pltpu.VMEM((blks, chunk, 2 * cols), f32),
            pltpu.VMEM((cols, 2 * cols), f32),
        ]
        panel_sems = pltpu.SemaphoreType.DMA((2, panels))
        blk_sems = pltpu.SemaphoreType.DMA((2, blks))
        outs = pl.pallas_call(
            functools.partial(kernel, panels, blks),
            out_shape=(out, out, out),
            in_specs=[vmem, vmem],
            out_specs=(vmem, vmem, vmem),
            scratch_shapes=[
                pltpu.VMEM((panels, rows, depth), bf16),
                pltpu.VMEM((blks, rows, depth), bf16),
                pltpu.VMEM((blks, cols, rows), bf16),
                pltpu.VMEM((panels, cols, rows), f32),
                pltpu.VMEM((panels, cols, rows), f32),
                *small,
                *small,
                pltpu.VMEM((cols, rows), f32),
                panel_sems,
                blk_sems,
                blk_sems,
                panel_sems,
                panel_sems,
                blk_sems,
                panel_sems,
                panel_sems,
                blk_sems,
                panel_sems,
            ],
            compiler_params=pltpu.CompilerParams(
                collective_id=0, has_side_effects=True, vmem_limit_bytes=48 * 1024 * 1024
            ),
        )(points, targets.T)
        return tuple(value.T for value in outs)

    placed = P(("groups", "blk", "panel"), None)
    return jax.shard_map(
        local,
        mesh=mesh,
        in_specs=(placed, placed),
        out_specs=(placed, placed, placed),
        check_vma=False,
    )
```

```python
import functools

import jax
import jax.numpy as jnp
from jax import lax
from jax.experimental import pallas as pl
from jax.experimental.pallas import tpu as pltpu
from jax.sharding import PartitionSpec as P

MESH = pl.DeviceIdType.MESH
HIGHEST = lax.Precision.HIGHEST
STEP = 8


def each(count, body):
    if count <= 16:
        for offset in range(1, count):
            body(offset)
    else:
        lax.fori_loop(1, count, lambda offset, carry: (body(offset), carry)[1], 0)


def dot_nt(a, b, precision=None):
    return lax.dot_general(
        a, b, (((1,), (1,)), ((), ())), precision=precision, preferred_element_type=jnp.float32
    )


def dot(a, b, precision=HIGHEST):
    return jnp.dot(a, b, precision=precision, preferred_element_type=jnp.float32)


def eliminate(whole, rows):
    width = whole.shape[1]
    blocks = [whole[i : i + STEP, :] for i in range(0, rows, STEP)]
    sub = lax.broadcasted_iota(jnp.int32, (STEP, width), 0)
    for k in range(rows // STEP):
        lead = blocks[k]
        spread = [
            [
                jnp.broadcast_to(block[:, k * STEP + j : k * STEP + j + 1], (STEP, width))
                for j in range(STEP)
            ]
            for block in blocks
        ]
        cols = list(spread[k])
        scales = jnp.ones((STEP, width), jnp.float32)
        for j in range(STEP):
            inverse = 1.0 / jnp.broadcast_to(cols[j][j : j + 1, :], (STEP, width))
            factor = jnp.where(sub == j, 0.0, cols[j] * inverse)
            scales = jnp.where(sub == j, inverse, scales)
            lead = lead - factor * jnp.broadcast_to(lead[j : j + 1, :], (STEP, width))
            for i in range(j + 1, STEP):
                cols[i] = cols[i] - factor * jnp.broadcast_to(cols[i][j : j + 1, :], (STEP, width))
        lead = lead * scales
        lead_rows = [jnp.broadcast_to(lead[j : j + 1, :], (STEP, width)) for j in range(STEP)]
        for i in range(rows // STEP):
            if i == k:
                blocks[i] = lead
            else:
                total = spread[i][0] * lead_rows[0]
                for j in range(1, STEP):
                    total = total + spread[i][j] * lead_rows[j]
                blocks[i] = blocks[i] - total
    return jnp.concatenate(blocks, axis=0)


def pack(value):
    half = value.shape[0] // 2
    return jnp.concatenate([value[:half], value[half:]], axis=1)


def unpack(value):
    half = value.shape[1] // 2
    return jnp.concatenate([value[:, :half], value[:, half:]], axis=0)


def kernel(
    panels,
    blks,
    points_ref,
    targets_ref,
    solution_ref,
    residual_ref,
    direction_ref,
    queries,
    keys,
    dirs,
    heights,
    parts,
    part_in,
    gram_panel,
    gram_blk,
    curv_panel,
    curv_blk,
    quad_panel,
    quad_blk,
    query_sems,
    key_sems,
    dir_sems,
    height_sems,
    part_sems,
    gram_panel_sems,
    gram_blk_sems,
    curv_panel_sems,
    curv_blk_sems,
    quad_panel_sems,
    quad_blk_sems,
    load_sems,
):
    rows, depth = points_ref.shape
    cols = targets_ref.shape[0]
    my_panel = lax.axis_index("panel")
    my_blk = lax.axis_index("blk")
    scale = 2.0 / depth

    def panel_at(offset):
        return {"panel": lax.rem(my_panel + offset, panels)}

    def blk_at(offset):
        return {"blk": lax.rem(my_blk + offset, blks)}

    def send(source, target, sems, index, device):
        return pltpu.make_async_remote_copy(
            src_ref=source,
            dst_ref=target,
            send_sem=sems.at[0, index],
            recv_sem=sems.at[1, index],
            device_id=device,
            device_id_type=MESH,
        )

    def panel_copy(buffer, sems, d):
        return send(buffer.at[0], buffer.at[d], sems, d, panel_at(d))

    def blk_copy(buffer, sems, d):
        return send(buffer.at[0], buffer.at[d], sems, d, blk_at(d))

    def over_panel(value, buffer, sems):
        buffer[0] = value
        each(panels, lambda d: panel_copy(buffer, sems, d).start())

    def over_blk(panel_buffer, panel_sems, buffer, sems):
        each(panels, lambda d: panel_copy(panel_buffer, panel_sems, d).wait())
        buffer[0] = jnp.sum(panel_buffer[...], axis=0)
        each(blks, lambda d: blk_copy(buffer, sems, d).start())

    def summed(buffer, sems):
        each(blks, lambda d: blk_copy(buffer, sems, d).wait())
        return unpack(jnp.sum(buffer[...], axis=0))

    barrier = pltpu.get_barrier_semaphore()
    each(blks, lambda d: pl.semaphore_signal(barrier, inc=1, device_id=blk_at(d), device_id_type=MESH))
    each(panels, lambda d: pl.semaphore_signal(barrier, inc=1, device_id=panel_at(d), device_id_type=MESH))
    load_targets = pltpu.make_async_copy(targets_ref, heights.at[0], load_sems.at[0])
    load_points = pltpu.make_async_copy(points_ref, queries.at[0], load_sems.at[1])
    load_targets.start()
    load_points.start()
    load_targets.wait()
    targets_t = heights[0]
    dirs[0] = targets_t.astype(jnp.bfloat16)
    own_gram = pack(dot_nt(targets_t, targets_t, HIGHEST))
    load_points.wait()

    def key_copy(d):
        return send(queries.at[0], keys.at[d], key_sems, d, blk_at(d))

    pl.semaphore_wait(barrier, panels - 1 + blks - 1)
    each(blks, lambda d: key_copy(d).start())
    each(blks, lambda d: blk_copy(dirs, dir_sems, d).start())
    each(panels, lambda d: panel_copy(queries, query_sems, d).start())
    over_panel(own_gram, gram_panel, gram_panel_sems)
    each(panels, lambda d: panel_copy(heights, height_sems, d).start())

    each(panels, lambda d: panel_copy(queries, query_sems, d).wait())
    over_blk(gram_panel, gram_panel_sems, gram_blk, gram_blk_sems)
    all_queries = queries[...].reshape(panels * rows, depth)
    wide = all_queries.astype(jnp.float32)
    sq_queries = dot_nt(jnp.full((8, depth), scale, jnp.float32), wide * wide, HIGHEST)[0:1, :]

    def tile(key, dir_piece):
        wide_key = key.astype(jnp.float32)
        sq_key = jnp.sum(wide_key * wide_key, axis=1, keepdims=True) * scale
        cross = dot_nt(key, all_queries)
        weight = jnp.exp(jnp.minimum((2.0 * scale) * cross - sq_key - sq_queries, 0.0)).astype(jnp.bfloat16)
        return jnp.dot(dir_piece, weight, preferred_element_type=jnp.float32)

    first = tile(queries[0], dirs[0])
    for p in range(panels):
        parts[p] = first[:, p * rows : (p + 1) * rows]

    def more(d):
        key_copy(d).wait()
        blk_copy(dirs, dir_sems, d).wait()
        value = tile(keys[d], dirs[d])
        for p in range(panels):
            parts[p] += value[:, p * rows : (p + 1) * rows]

    each(blks, more)

    def part_copy(d):
        return send(parts.at[d], part_in.at[d], part_sems, d, panel_at(panels - d))

    each(panels, lambda d: part_copy(d).start())
    each(panels, lambda d: panel_copy(heights, height_sems, d).wait())
    own_curv = dot_nt(parts[0], heights[0], HIGHEST)
    for p in range(1, panels):
        own_curv = own_curv + dot_nt(parts[p], heights[p], HIGHEST)
    over_panel(pack(own_curv), curv_panel, curv_panel_sems)

    lane = lax.broadcasted_iota(jnp.int32, (cols, 2 * cols), 1)
    line = lax.broadcasted_iota(jnp.int32, (cols, 2 * cols), 0)
    gram = summed(gram_blk, gram_blk_sems)
    twice = jnp.concatenate([gram, gram], axis=1)
    unit = (lane == line + cols).astype(jnp.float32)
    gram_inv = eliminate(jnp.where(lane < cols, twice, unit), cols)[:, cols:]
    solved = dot(gram_inv, targets_t)

    each(panels, lambda d: part_copy(d).wait())
    part_in[0] = parts[0]
    image_t = 1.0 * targets_t + jnp.sum(part_in[...], axis=0)
    over_panel(pack(dot_nt(image_t, image_t, HIGHEST)), quad_panel, quad_panel_sems)
    over_blk(curv_panel, curv_panel_sems, curv_blk, curv_blk_sems)
    over_blk(quad_panel, quad_panel_sems, quad_blk, quad_blk_sems)
    curv_t = gram + summed(curv_blk, curv_blk_sems)
    curv = curv_t.T
    symmetric = 0.5 * (curv + curv_t)
    start = jnp.concatenate([symmetric, gram], axis=1)
    alpha_t = eliminate(start, cols)[:, cols:].T
    made = dot(alpha_t, jnp.concatenate([targets_t, image_t], axis=1))
    residual = targets_t - made[:, rows:]
    solution_ref[...] = made[:, :rows]
    residual_ref[...] = residual
    known = gram - dot(alpha_t, curv_t) - dot_nt(curv, alpha_t, HIGHEST)
    moved = dot(alpha_t.T, solved)
    base = residual + dot(known, solved)
    quad = summed(quad_blk, quad_blk_sems)
    direction_ref[...] = base + dot(alpha_t, dot(quad, moved))


def solution(mesh):
    panels, blks = mesh.shape["panel"], mesh.shape["blk"]

    def local(points, targets):
        rows, depth = points.shape
        cols = targets.shape[1]
        f32, bf16 = jnp.float32, jnp.bfloat16
        out = jax.ShapeDtypeStruct((cols, rows), f32)
        vmem = pl.BlockSpec(memory_space=pltpu.VMEM)
        small = [pltpu.VMEM((panels, cols // 2, 2 * cols), f32), pltpu.VMEM((blks, cols // 2, 2 * cols), f32)]
        panel_sems = pltpu.SemaphoreType.DMA((2, panels))
        blk_sems = pltpu.SemaphoreType.DMA((2, blks))
        outs = pl.pallas_call(
            functools.partial(kernel, panels, blks),
            out_shape=(out, out, out),
            in_specs=[pl.BlockSpec(memory_space=pl.ANY)] * 2,
            out_specs=(vmem, vmem, vmem),
            scratch_shapes=[
                pltpu.VMEM((panels, rows, depth), bf16),
                pltpu.VMEM((blks, rows, depth), bf16),
                pltpu.VMEM((blks, cols, rows), bf16),
                pltpu.VMEM((panels, cols, rows), f32),
                pltpu.VMEM((panels, cols, rows), f32),
                pltpu.VMEM((panels, cols, rows), f32),
                *small,
                *small,
                *small,
                panel_sems,
                blk_sems,
                blk_sems,
                panel_sems,
                panel_sems,
                panel_sems,
                blk_sems,
                panel_sems,
                blk_sems,
                panel_sems,
                blk_sems,
                pltpu.SemaphoreType.DMA((2,)),
            ],
            compiler_params=pltpu.CompilerParams(collective_id=0, has_side_effects=True),
        )(points, targets.T)
        return tuple(value.T for value in outs)

    placed = P(("groups", "blk", "panel"), None)
    return jax.shard_map(
        local,
        mesh=mesh,
        in_specs=(placed, placed),
        out_specs=(placed, placed, placed),
        check_vma=False,
    )
```

```python
import functools

import jax
import jax.numpy as jnp
from jax import lax
from jax.experimental import pallas as pl
from jax.experimental.pallas import tpu as pltpu
from jax.sharding import PartitionSpec as P

MESH = pl.DeviceIdType.MESH
HIGHEST = lax.Precision.HIGHEST
STEP = 8


def each(count, body):
    if count <= 16:
        for offset in range(1, count):
            body(offset)
    else:
        lax.fori_loop(1, count, lambda offset, carry: (body(offset), carry)[1], 0)


def dot_nt(a, b, precision=None):
    return lax.dot_general(
        a, b, (((1,), (1,)), ((), ())), precision=precision, preferred_element_type=jnp.float32
    )


def dot(a, b, precision=HIGHEST):
    return jnp.dot(a, b, precision=precision, preferred_element_type=jnp.float32)


def eliminate(whole, rows):
    width = whole.shape[1]
    blocks = [whole[i : i + STEP, :] for i in range(0, rows, STEP)]
    sub = lax.broadcasted_iota(jnp.int32, (STEP, width), 0)
    for k in range(rows // STEP):
        lead = blocks[k]
        spread = [
            [
                jnp.broadcast_to(block[:, k * STEP + j : k * STEP + j + 1], (STEP, width))
                for j in range(STEP)
            ]
            for block in blocks
        ]
        cols = list(spread[k])
        scales = jnp.ones((STEP, width), jnp.float32)
        for j in range(STEP):
            inverse = 1.0 / jnp.broadcast_to(cols[j][j : j + 1, :], (STEP, width))
            factor = jnp.where(sub == j, 0.0, cols[j] * inverse)
            scales = jnp.where(sub == j, inverse, scales)
            lead = lead - factor * jnp.broadcast_to(lead[j : j + 1, :], (STEP, width))
            for i in range(j + 1, STEP):
                cols[i] = cols[i] - factor * jnp.broadcast_to(cols[i][j : j + 1, :], (STEP, width))
        lead = lead * scales
        lead_rows = [jnp.broadcast_to(lead[j : j + 1, :], (STEP, width)) for j in range(STEP)]
        for i in range(rows // STEP):
            if i == k:
                blocks[i] = lead
            else:
                total = spread[i][0] * lead_rows[0]
                for j in range(1, STEP):
                    total = total + spread[i][j] * lead_rows[j]
                blocks[i] = blocks[i] - total
    return jnp.concatenate(blocks, axis=0)


def pack(value):
    half = value.shape[0] // 2
    return jnp.concatenate([value[:half], value[half:]], axis=1)


def unpack(value):
    half = value.shape[1] // 2
    return jnp.concatenate([value[:, :half], value[:, half:]], axis=0)


def kernel(
    panels,
    blks,
    points_ref,
    targets_ref,
    solution_ref,
    residual_ref,
    direction_ref,
    queries,
    keys,
    dirs,
    heights,
    parts,
    part_in,
    gram_panel,
    gram_blk,
    curv_panel,
    curv_blk,
    quad_panel,
    quad_blk,
    query_sems,
    key_sems,
    dir_sems,
    height_sems,
    part_sems,
    gram_panel_sems,
    gram_blk_sems,
    curv_panel_sems,
    curv_blk_sems,
    quad_panel_sems,
    quad_blk_sems,
    load_sems,
):
    rows, depth = points_ref.shape
    cols = targets_ref.shape[0]
    my_panel = lax.axis_index("panel")
    my_blk = lax.axis_index("blk")
    scale = 2.0 / depth

    def panel_at(offset):
        return {"panel": lax.rem(my_panel + offset, panels)}

    def blk_at(offset):
        return {"blk": lax.rem(my_blk + offset, blks)}

    def send(source, target, sems, index, device):
        return pltpu.make_async_remote_copy(
            src_ref=source,
            dst_ref=target,
            send_sem=sems.at[0, index],
            recv_sem=sems.at[1, index],
            device_id=device,
            device_id_type=MESH,
        )

    def panel_copy(buffer, sems, d):
        return send(buffer.at[0], buffer.at[d], sems, d, panel_at(d))

    def blk_copy(buffer, sems, d):
        return send(buffer.at[0], buffer.at[d], sems, d, blk_at(d))

    def over_panel(value, buffer, sems):
        buffer[0] = value
        each(panels, lambda d: panel_copy(buffer, sems, d).start())

    def over_blk(panel_buffer, panel_sems, buffer, sems):
        each(panels, lambda d: panel_copy(panel_buffer, panel_sems, d).wait())
        buffer[0] = jnp.sum(panel_buffer[...], axis=0)
        each(blks, lambda d: blk_copy(buffer, sems, d).start())

    def summed(buffer, sems):
        each(blks, lambda d: blk_copy(buffer, sems, d).wait())
        return unpack(jnp.sum(buffer[...], axis=0))

    barrier = pltpu.get_barrier_semaphore()
    each(blks, lambda d: pl.semaphore_signal(barrier, inc=1, device_id=blk_at(d), device_id_type=MESH))
    each(panels, lambda d: pl.semaphore_signal(barrier, inc=1, device_id=panel_at(d), device_id_type=MESH))
    load_targets = pltpu.make_async_copy(targets_ref, heights.at[0], load_sems.at[0])
    load_points = pltpu.make_async_copy(points_ref, queries.at[0], load_sems.at[1])
    load_targets.start()
    load_points.start()
    load_targets.wait()
    targets_t = heights[0]
    dirs[0] = targets_t.astype(jnp.bfloat16)
    own_gram = pack(dot_nt(targets_t, targets_t, HIGHEST))
    load_points.wait()

    def key_copy(d):
        return send(queries.at[0], keys.at[d], key_sems, d, blk_at(d))

    pl.semaphore_wait(barrier, panels - 1 + blks - 1)
    each(blks, lambda d: key_copy(d).start())
    each(blks, lambda d: blk_copy(dirs, dir_sems, d).start())
    each(panels, lambda d: panel_copy(queries, query_sems, d).start())
    over_panel(own_gram, gram_panel, gram_panel_sems)
    each(panels, lambda d: panel_copy(heights, height_sems, d).start())

    each(panels, lambda d: panel_copy(queries, query_sems, d).wait())
    all_queries = queries[...].reshape(panels * rows, depth)
    wide = all_queries.astype(jnp.float32)
    sq_queries = dot_nt(jnp.full((8, depth), scale, jnp.float32), wide * wide, HIGHEST)[0:1, :]

    def tile(key, dir_piece):
        wide_key = key.astype(jnp.float32)
        sq_key = jnp.sum(wide_key * wide_key, axis=1, keepdims=True) * scale
        cross = dot_nt(key, all_queries)
        weight = jnp.exp(jnp.minimum((2.0 * scale) * cross - sq_key - sq_queries, 0.0)).astype(jnp.bfloat16)
        return jnp.dot(dir_piece, weight, preferred_element_type=jnp.float32)

    first = tile(queries[0], dirs[0])
    for p in range(panels):
        parts[p] = first[:, p * rows : (p + 1) * rows]

    def more(d):
        key_copy(d).wait()
        blk_copy(dirs, dir_sems, d).wait()
        value = tile(keys[d], dirs[d])
        for p in range(panels):
            parts[p] += value[:, p * rows : (p + 1) * rows]

    each(blks, more)

    def part_copy(d):
        return send(parts.at[d], part_in.at[d], part_sems, d, panel_at(panels - d))

    each(panels, lambda d: part_copy(d).start())
    over_blk(gram_panel, gram_panel_sems, gram_blk, gram_blk_sems)
    each(panels, lambda d: panel_copy(heights, height_sems, d).wait())
    own_curv = dot_nt(parts[0], heights[0], HIGHEST)
    for p in range(1, panels):
        own_curv = own_curv + dot_nt(parts[p], heights[p], HIGHEST)
    over_panel(pack(own_curv), curv_panel, curv_panel_sems)

    each(panels, lambda d: part_copy(d).wait())
    part_in[0] = parts[0]
    image_t = 1.0 * targets_t + jnp.sum(part_in[...], axis=0)
    over_panel(pack(dot_nt(image_t, image_t, HIGHEST)), quad_panel, quad_panel_sems)
    over_blk(curv_panel, curv_panel_sems, curv_blk, curv_blk_sems)
    lane = lax.broadcasted_iota(jnp.int32, (cols, 2 * cols), 1)
    line = lax.broadcasted_iota(jnp.int32, (cols, 2 * cols), 0)
    gram = summed(gram_blk, gram_blk_sems)
    twice = jnp.concatenate([gram, gram], axis=1)
    unit = (lane == line + cols).astype(jnp.float32)
    gram_inv = eliminate(jnp.where(lane < cols, twice, unit), cols)[:, cols:]
    solved = dot(gram_inv, targets_t)

    over_blk(quad_panel, quad_panel_sems, quad_blk, quad_blk_sems)
    curv_t = gram + summed(curv_blk, curv_blk_sems)
    curv = curv_t.T
    symmetric = 0.5 * (curv + curv_t)
    start = jnp.concatenate([symmetric, gram], axis=1)
    alpha_t = eliminate(start, cols)[:, cols:].T
    made = dot(alpha_t, jnp.concatenate([targets_t, image_t], axis=1))
    residual = targets_t - made[:, rows:]
    solution_ref[...] = made[:, :rows]
    residual_ref[...] = residual
    known = gram - dot(alpha_t, curv_t) - dot_nt(curv, alpha_t, HIGHEST)
    moved = dot(alpha_t.T, solved)
    base = residual + dot(known, solved)
    quad = summed(quad_blk, quad_blk_sems)
    direction_ref[...] = base + dot(alpha_t, dot(quad, moved))


def write(solution_ref, residual_ref, direction_ref, *outs):
    for source, out in zip((solution_ref, residual_ref, direction_ref), outs):
        out[...] = source[...]


def solution(mesh):
    panels, blks = mesh.shape["panel"], mesh.shape["blk"]

    def local(points, targets):
        rows, depth = points.shape
        cols = targets.shape[1]
        f32, bf16 = jnp.float32, jnp.bfloat16
        out = jax.ShapeDtypeStruct((cols, rows), f32)
        vmem = pl.BlockSpec(memory_space=pltpu.VMEM)
        small = [pltpu.VMEM((panels, cols // 2, 2 * cols), f32), pltpu.VMEM((blks, cols // 2, 2 * cols), f32)]
        panel_sems = pltpu.SemaphoreType.DMA((2, panels))
        blk_sems = pltpu.SemaphoreType.DMA((2, blks))
        outs = pl.pallas_call(
            functools.partial(kernel, panels, blks),
            out_shape=(out, out, out),
            in_specs=[pl.BlockSpec(memory_space=pl.ANY)] * 2,
            out_specs=(vmem, vmem, vmem),
            scratch_shapes=[
                pltpu.VMEM((panels, rows, depth), bf16),
                pltpu.VMEM((blks, rows, depth), bf16),
                pltpu.VMEM((blks, cols, rows), bf16),
                pltpu.VMEM((panels, cols, rows), f32),
                pltpu.VMEM((panels, cols, rows), f32),
                pltpu.VMEM((panels, cols, rows), f32),
                *small,
                *small,
                *small,
                panel_sems,
                blk_sems,
                blk_sems,
                panel_sems,
                panel_sems,
                panel_sems,
                blk_sems,
                panel_sems,
                blk_sems,
                panel_sems,
                blk_sems,
                pltpu.SemaphoreType.DMA((2,)),
            ],
            compiler_params=pltpu.CompilerParams(collective_id=0, has_side_effects=True),
        )(points, targets.T)
        done = pl.pallas_call(write, out_shape=(out, out, out), in_specs=[vmem] * 3, out_specs=(vmem,) * 3)(*outs)
        return tuple(value.T for value in done)

    placed = P(("groups", "blk", "panel"), None)
    return jax.shard_map(
        local,
        mesh=mesh,
        in_specs=(placed, placed),
        out_specs=(placed, placed, placed),
        check_vma=False,
    )
```

```python
import functools

import jax
import jax.numpy as jnp
from jax import lax
from jax.experimental import pallas as pl
from jax.experimental.pallas import tpu as pltpu
from jax.sharding import PartitionSpec as P

MESH = pl.DeviceIdType.MESH
HIGHEST = lax.Precision.HIGHEST
STEP = 8


def each(count, body):
    if count <= 16:
        for offset in range(1, count):
            body(offset)
    else:
        lax.fori_loop(1, count, lambda offset, carry: (body(offset), carry)[1], 0)


def dot_nt(a, b, precision=None):
    return lax.dot_general(
        a, b, (((1,), (1,)), ((), ())), precision=precision, preferred_element_type=jnp.float32
    )


def dot(a, b, precision=HIGHEST):
    return jnp.dot(a, b, precision=precision, preferred_element_type=jnp.float32)


def eliminate(whole, rows):
    width = whole.shape[1]
    blocks = [whole[i : i + STEP, :] for i in range(0, rows, STEP)]
    sub = lax.broadcasted_iota(jnp.int32, (STEP, width), 0)
    for k in range(rows // STEP):
        lead = blocks[k]
        spread = [
            [
                jnp.broadcast_to(block[:, k * STEP + j : k * STEP + j + 1], (STEP, width))
                for j in range(STEP)
            ]
            for block in blocks
        ]
        cols = list(spread[k])
        scales = jnp.ones((STEP, width), jnp.float32)
        for j in range(STEP):
            inverse = 1.0 / jnp.broadcast_to(cols[j][j : j + 1, :], (STEP, width))
            factor = jnp.where(sub == j, 0.0, cols[j] * inverse)
            scales = jnp.where(sub == j, inverse, scales)
            lead = lead - factor * jnp.broadcast_to(lead[j : j + 1, :], (STEP, width))
            for i in range(j + 1, STEP):
                cols[i] = cols[i] - factor * jnp.broadcast_to(cols[i][j : j + 1, :], (STEP, width))
        lead = lead * scales
        lead_rows = [jnp.broadcast_to(lead[j : j + 1, :], (STEP, width)) for j in range(STEP)]
        for i in range(rows // STEP):
            if i == k:
                blocks[i] = lead
            else:
                total = spread[i][0] * lead_rows[0]
                for j in range(1, STEP):
                    total = total + spread[i][j] * lead_rows[j]
                blocks[i] = blocks[i] - total
    return jnp.concatenate(blocks, axis=0)


def pack(value):
    half = value.shape[0] // 2
    return jnp.concatenate([value[:half], value[half:]], axis=1)


def unpack(value):
    half = value.shape[1] // 2
    return jnp.concatenate([value[:, :half], value[:, half:]], axis=0)


def kernel(
    panels,
    blks,
    points_ref,
    targets_ref,
    solution_ref,
    residual_ref,
    direction_ref,
    queries,
    keys,
    dirs,
    heights,
    parts,
    part_in,
    gram_panel,
    gram_blk,
    curv_panel,
    curv_blk,
    quad_panel,
    quad_blk,
    query_sems,
    key_sems,
    dir_sems,
    height_sems,
    part_sems,
    gram_panel_sems,
    gram_blk_sems,
    curv_panel_sems,
    curv_blk_sems,
    quad_panel_sems,
    quad_blk_sems,
    load_sems,
):
    rows, depth = points_ref.shape
    cols = targets_ref.shape[0]
    my_panel = lax.axis_index("panel")
    my_blk = lax.axis_index("blk")
    scale = 2.0 / depth

    def panel_at(offset):
        return {"panel": lax.rem(my_panel + offset, panels)}

    def blk_at(offset):
        return {"blk": lax.rem(my_blk + offset, blks)}

    def send(source, target, sems, index, device):
        return pltpu.make_async_remote_copy(
            src_ref=source,
            dst_ref=target,
            send_sem=sems.at[0, index],
            recv_sem=sems.at[1, index],
            device_id=device,
            device_id_type=MESH,
        )

    def panel_copy(buffer, sems, d):
        return send(buffer.at[0], buffer.at[d], sems, d, panel_at(d))

    def blk_copy(buffer, sems, d):
        return send(buffer.at[0], buffer.at[d], sems, d, blk_at(d))

    def over_panel(value, buffer, sems):
        buffer[0] = value
        each(panels, lambda d: panel_copy(buffer, sems, d).start())

    def over_blk(panel_buffer, panel_sems, buffer, sems):
        each(panels, lambda d: panel_copy(panel_buffer, panel_sems, d).wait())
        buffer[0] = jnp.sum(panel_buffer[...], axis=0)
        each(blks, lambda d: blk_copy(buffer, sems, d).start())

    def summed(buffer, sems):
        each(blks, lambda d: blk_copy(buffer, sems, d).wait())
        return unpack(jnp.sum(buffer[...], axis=0))

    barrier = pltpu.get_barrier_semaphore()
    each(blks, lambda d: pl.semaphore_signal(barrier, inc=1, device_id=blk_at(d), device_id_type=MESH))
    each(panels, lambda d: pl.semaphore_signal(barrier, inc=1, device_id=panel_at(d), device_id_type=MESH))
    load_targets = pltpu.make_async_copy(targets_ref, heights.at[0], load_sems.at[0])
    load_points = pltpu.make_async_copy(points_ref, queries.at[0], load_sems.at[1])
    load_targets.start()
    load_points.start()
    load_targets.wait()
    targets_t = heights[0]
    dirs[0] = targets_t.astype(jnp.bfloat16)
    own_gram = pack(dot_nt(targets_t, targets_t, HIGHEST))
    load_points.wait()

    def key_copy(d):
        return send(queries.at[0], keys.at[d], key_sems, d, blk_at(d))

    pl.semaphore_wait(barrier, panels - 1 + blks - 1)
    each(blks, lambda d: key_copy(d).start())
    each(blks, lambda d: blk_copy(dirs, dir_sems, d).start())
    each(panels, lambda d: panel_copy(queries, query_sems, d).start())
    over_panel(own_gram, gram_panel, gram_panel_sems)
    each(panels, lambda d: panel_copy(heights, height_sems, d).start())

    each(panels, lambda d: panel_copy(queries, query_sems, d).wait())
    all_queries = queries[...].reshape(panels * rows, depth)
    wide = all_queries.astype(jnp.float32)
    sq_queries = dot_nt(jnp.full((8, depth), scale, jnp.float32), wide * wide, HIGHEST)[0:1, :]

    def tile(key, dir_piece):
        wide_key = key.astype(jnp.float32)
        sq_key = jnp.sum(wide_key * wide_key, axis=1, keepdims=True) * scale
        cross = dot_nt(key, all_queries)
        weight = jnp.exp(jnp.minimum((2.0 * scale) * cross - sq_key - sq_queries, 0.0)).astype(jnp.bfloat16)
        return jnp.dot(dir_piece, weight, preferred_element_type=jnp.float32)

    first = tile(queries[0], dirs[0])
    for p in range(panels):
        parts[p] = first[:, p * rows : (p + 1) * rows]

    def more(d):
        key_copy(d).wait()
        blk_copy(dirs, dir_sems, d).wait()
        value = tile(keys[d], dirs[d])
        for p in range(panels):
            parts[p] += value[:, p * rows : (p + 1) * rows]

    each(blks, more)

    def part_copy(d):
        return send(parts.at[d], part_in.at[d], part_sems, d, panel_at(panels - d))

    each(panels, lambda d: part_copy(d).start())
    over_blk(gram_panel, gram_panel_sems, gram_blk, gram_blk_sems)
    each(panels, lambda d: panel_copy(heights, height_sems, d).wait())
    own_curv = dot_nt(parts[0], heights[0], HIGHEST)
    for p in range(1, panels):
        own_curv = own_curv + dot_nt(parts[p], heights[p], HIGHEST)
    over_panel(pack(own_curv), curv_panel, curv_panel_sems)

    each(panels, lambda d: part_copy(d).wait())
    part_in[0] = parts[0]
    image_t = 1.0 * targets_t + jnp.sum(part_in[...], axis=0)
    over_panel(pack(dot_nt(image_t, image_t, HIGHEST)), quad_panel, quad_panel_sems)
    over_blk(curv_panel, curv_panel_sems, curv_blk, curv_blk_sems)
    lane = lax.broadcasted_iota(jnp.int32, (cols, 2 * cols), 1)
    line = lax.broadcasted_iota(jnp.int32, (cols, 2 * cols), 0)
    gram = summed(gram_blk, gram_blk_sems)
    twice = jnp.concatenate([gram, gram], axis=1)
    unit = (lane == line + cols).astype(jnp.float32)
    gram_inv = eliminate(jnp.where(lane < cols, twice, unit), cols)[:, cols:]
    solved = dot(gram_inv, targets_t)

    over_blk(quad_panel, quad_panel_sems, quad_blk, quad_blk_sems)
    curv_t = gram + summed(curv_blk, curv_blk_sems)
    curv = curv_t.T
    symmetric = 0.5 * (curv + curv_t)
    start = jnp.concatenate([symmetric, gram], axis=1)
    alpha = eliminate(start, cols)[:, cols:]
    alpha_t = alpha.T
    moved = dot(alpha, solved)
    quad = summed(quad_blk, quad_blk_sems)
    squared = dot(alpha_t, dot(quad, moved))
    made = dot(alpha_t, jnp.concatenate([targets_t, image_t], axis=1))
    residual = targets_t - made[:, rows:]
    known = gram - dot(alpha_t, curv_t) - dot_nt(curv, alpha_t, HIGHEST)
    solution_ref[...] = made[:, :rows]
    residual_ref[...] = residual
    direction_ref[...] = residual + dot(known, solved) + squared


def write(solution_ref, residual_ref, direction_ref, *outs):
    for source, out in zip((solution_ref, residual_ref, direction_ref), outs):
        out[...] = source[...]


def solution(mesh):
    panels, blks = mesh.shape["panel"], mesh.shape["blk"]

    def local(points, targets):
        rows, depth = points.shape
        cols = targets.shape[1]
        f32, bf16 = jnp.float32, jnp.bfloat16
        out = jax.ShapeDtypeStruct((cols, rows), f32)
        vmem = pl.BlockSpec(memory_space=pltpu.VMEM)
        small = [pltpu.VMEM((panels, cols // 2, 2 * cols), f32), pltpu.VMEM((blks, cols // 2, 2 * cols), f32)]
        panel_sems = pltpu.SemaphoreType.DMA((2, panels))
        blk_sems = pltpu.SemaphoreType.DMA((2, blks))
        outs = pl.pallas_call(
            functools.partial(kernel, panels, blks),
            out_shape=(out, out, out),
            in_specs=[pl.BlockSpec(memory_space=pl.ANY)] * 2,
            out_specs=(vmem, vmem, vmem),
            scratch_shapes=[
                pltpu.VMEM((panels, rows, depth), bf16),
                pltpu.VMEM((blks, rows, depth), bf16),
                pltpu.VMEM((blks, cols, rows), bf16),
                pltpu.VMEM((panels, cols, rows), f32),
                pltpu.VMEM((panels, cols, rows), f32),
                pltpu.VMEM((panels, cols, rows), f32),
                *small,
                *small,
                *small,
                panel_sems,
                blk_sems,
                blk_sems,
                panel_sems,
                panel_sems,
                panel_sems,
                blk_sems,
                panel_sems,
                blk_sems,
                panel_sems,
                blk_sems,
                pltpu.SemaphoreType.DMA((2,)),
            ],
            compiler_params=pltpu.CompilerParams(collective_id=0, has_side_effects=True),
        )(points, targets.T)
        done = pl.pallas_call(write, out_shape=(out, out, out), in_specs=[vmem] * 3, out_specs=(vmem,) * 3)(*outs)
        return tuple(value.T for value in done)

    placed = P(("groups", "blk", "panel"), None)
    return jax.shard_map(
        local,
        mesh=mesh,
        in_specs=(placed, placed),
        out_specs=(placed, placed, placed),
        check_vma=False,
    )
```

```python
import functools

import jax
import jax.numpy as jnp
from jax import lax
from jax.experimental import pallas as pl
from jax.experimental.pallas import tpu as pltpu
from jax.sharding import PartitionSpec as P

MESH = pl.DeviceIdType.MESH
HIGHEST = lax.Precision.HIGHEST
STEP = 8


def each(count, body):
    if count <= 16:
        for offset in range(1, count):
            body(offset)
    else:
        lax.fori_loop(1, count, lambda offset, carry: (body(offset), carry)[1], 0)


def dot_nt(a, b, precision=None):
    return lax.dot_general(
        a, b, (((1,), (1,)), ((), ())), precision=precision, preferred_element_type=jnp.float32
    )


def dot(a, b, precision=HIGHEST):
    return jnp.dot(a, b, precision=precision, preferred_element_type=jnp.float32)


def eliminate(whole, rows):
    width = whole.shape[1]
    blocks = [whole[i : i + STEP, :] for i in range(0, rows, STEP)]
    sub = lax.broadcasted_iota(jnp.int32, (STEP, width), 0)
    for k in range(rows // STEP):
        lead = blocks[k]
        spread = [
            [
                jnp.broadcast_to(block[:, k * STEP + j : k * STEP + j + 1], (STEP, width))
                for j in range(STEP)
            ]
            for block in blocks
        ]
        cols = list(spread[k])
        scales = jnp.ones((STEP, width), jnp.float32)
        for j in range(STEP):
            inverse = 1.0 / jnp.broadcast_to(cols[j][j : j + 1, :], (STEP, width))
            factor = jnp.where(sub == j, 0.0, cols[j] * inverse)
            scales = jnp.where(sub == j, inverse, scales)
            lead = lead - factor * jnp.broadcast_to(lead[j : j + 1, :], (STEP, width))
            for i in range(j + 1, STEP):
                cols[i] = cols[i] - factor * jnp.broadcast_to(cols[i][j : j + 1, :], (STEP, width))
        lead = lead * scales
        lead_rows = [jnp.broadcast_to(lead[j : j + 1, :], (STEP, width)) for j in range(STEP)]
        for i in range(rows // STEP):
            if i == k:
                blocks[i] = lead
            else:
                total = spread[i][0] * lead_rows[0]
                for j in range(1, STEP):
                    total = total + spread[i][j] * lead_rows[j]
                blocks[i] = blocks[i] - total
    return jnp.concatenate(blocks, axis=0)


def pack(value):
    half = value.shape[0] // 2
    return jnp.concatenate([value[:half], value[half:]], axis=1)


def unpack(value):
    half = value.shape[1] // 2
    return jnp.concatenate([value[:, :half], value[:, half:]], axis=0)


def kernel(
    panels,
    blks,
    points_ref,
    targets_ref,
    solution_ref,
    residual_ref,
    direction_ref,
    queries,
    keys,
    dirs,
    heights,
    parts,
    part_in,
    gram_panel,
    gram_blk,
    curv_panel,
    curv_blk,
    quad_panel,
    quad_blk,
    query_sems,
    key_sems,
    dir_sems,
    height_sems,
    part_sems,
    gram_panel_sems,
    gram_blk_sems,
    curv_panel_sems,
    curv_blk_sems,
    quad_panel_sems,
    quad_blk_sems,
    load_sems,
):
    rows, depth = points_ref.shape
    cols = targets_ref.shape[0]
    my_panel = lax.axis_index("panel")
    my_blk = lax.axis_index("blk")
    scale = 2.0 / depth

    def panel_at(offset):
        return {"panel": lax.rem(my_panel + offset, panels)}

    def blk_at(offset):
        return {"blk": lax.rem(my_blk + offset, blks)}

    def send(source, target, sems, index, device):
        return pltpu.make_async_remote_copy(
            src_ref=source,
            dst_ref=target,
            send_sem=sems.at[0, index],
            recv_sem=sems.at[1, index],
            device_id=device,
            device_id_type=MESH,
        )

    def panel_copy(buffer, sems, d):
        return send(buffer.at[0], buffer.at[d], sems, d, panel_at(d))

    def blk_copy(buffer, sems, d):
        return send(buffer.at[0], buffer.at[d], sems, d, blk_at(d))

    def over_panel(value, buffer, sems):
        buffer[0] = value
        each(panels, lambda d: panel_copy(buffer, sems, d).start())

    def over_blk(panel_buffer, panel_sems, buffer, sems):
        each(panels, lambda d: panel_copy(panel_buffer, panel_sems, d).wait())
        buffer[0] = jnp.sum(panel_buffer[...], axis=0)
        each(blks, lambda d: blk_copy(buffer, sems, d).start())

    def summed(buffer, sems):
        each(blks, lambda d: blk_copy(buffer, sems, d).wait())
        return unpack(jnp.sum(buffer[...], axis=0))

    barrier = pltpu.get_barrier_semaphore()
    each(blks, lambda d: pl.semaphore_signal(barrier, inc=1, device_id=blk_at(d), device_id_type=MESH))
    each(panels, lambda d: pl.semaphore_signal(barrier, inc=1, device_id=panel_at(d), device_id_type=MESH))
    load_targets = pltpu.make_async_copy(targets_ref, heights.at[0], load_sems.at[0])
    load_points = pltpu.make_async_copy(points_ref, queries.at[0], load_sems.at[1])
    load_targets.start()
    load_points.start()
    load_targets.wait()
    targets_t = heights[0]
    dirs[0] = targets_t.astype(jnp.bfloat16)
    own_gram = pack(dot_nt(targets_t, targets_t, HIGHEST))
    load_points.wait()

    def key_copy(d):
        return send(queries.at[0], keys.at[d], key_sems, d, blk_at(d))

    pl.semaphore_wait(barrier, panels - 1 + blks - 1)
    each(blks, lambda d: key_copy(d).start())
    each(blks, lambda d: blk_copy(dirs, dir_sems, d).start())
    each(panels, lambda d: panel_copy(queries, query_sems, d).start())
    over_panel(own_gram, gram_panel, gram_panel_sems)
    each(panels, lambda d: panel_copy(heights, height_sems, d).start())

    each(panels, lambda d: panel_copy(queries, query_sems, d).wait())
    all_queries = queries[...].reshape(panels * rows, depth)
    wide = all_queries.astype(jnp.float32)
    sq_queries = dot_nt(jnp.full((8, depth), scale, jnp.float32), wide * wide, HIGHEST)[0:1, :]

    def tile(key, dir_piece):
        wide_key = key.astype(jnp.float32)
        sq_key = jnp.sum(wide_key * wide_key, axis=1, keepdims=True) * scale
        cross = dot_nt(key, all_queries)
        weight = jnp.exp(jnp.minimum((2.0 * scale) * cross - sq_key - sq_queries, 0.0)).astype(jnp.bfloat16)
        return jnp.dot(dir_piece, weight, preferred_element_type=jnp.float32)

    first = tile(queries[0], dirs[0])
    for p in range(panels):
        parts[p] = first[:, p * rows : (p + 1) * rows]

    def more(d):
        key_copy(d).wait()
        blk_copy(dirs, dir_sems, d).wait()
        value = tile(keys[d], dirs[d])
        for p in range(panels):
            parts[p] += value[:, p * rows : (p + 1) * rows]

    each(blks, more)

    def part_copy(d):
        return send(parts.at[d], part_in.at[d], part_sems, d, panel_at(panels - d))

    each(panels, lambda d: part_copy(d).start())
    over_blk(gram_panel, gram_panel_sems, gram_blk, gram_blk_sems)
    each(panels, lambda d: panel_copy(heights, height_sems, d).wait())
    own_curv = dot_nt(parts[0], heights[0], HIGHEST)
    for p in range(1, panels):
        own_curv = own_curv + dot_nt(parts[p], heights[p], HIGHEST)
    over_panel(pack(own_curv), curv_panel, curv_panel_sems)

    each(panels, lambda d: part_copy(d).wait())
    part_in[0] = parts[0]
    image_t = 1.0 * targets_t + jnp.sum(part_in[...], axis=0)
    over_panel(pack(dot_nt(image_t, image_t, HIGHEST)), quad_panel, quad_panel_sems)
    over_blk(curv_panel, curv_panel_sems, curv_blk, curv_blk_sems)
    lane = lax.broadcasted_iota(jnp.int32, (cols, 2 * cols), 1)
    line = lax.broadcasted_iota(jnp.int32, (cols, 2 * cols), 0)
    gram = summed(gram_blk, gram_blk_sems)
    twice = jnp.concatenate([gram, gram], axis=1)
    unit = (lane == line + cols).astype(jnp.float32)
    gram_inv = eliminate(jnp.where(lane < cols, twice, unit), cols)[:, cols:]
    solved = dot(gram_inv, targets_t)

    over_blk(quad_panel, quad_panel_sems, quad_blk, quad_blk_sems)
    curv_t = gram + summed(curv_blk, curv_blk_sems)
    curv = curv_t.T
    symmetric = 0.5 * (curv + curv_t)
    start = jnp.concatenate([symmetric, gram], axis=1)
    alpha = eliminate(start, cols)[:, cols:]
    alpha_t = alpha.T
    moved = dot(alpha, solved)
    quad = summed(quad_blk, quad_blk_sems)
    squared = dot(alpha_t, dot(quad, moved))
    made = dot(alpha_t, jnp.concatenate([targets_t, image_t], axis=1))
    residual = targets_t - made[:, rows:]
    known = gram - dot(alpha_t, curv_t) - dot_nt(curv, alpha_t, HIGHEST)
    solution_ref[...] = made[:, :rows]
    residual_ref[...] = residual
    direction_ref[...] = residual + dot(known, solved) + squared


def write(solution_ref, residual_ref, direction_ref, solution_out, residual_out, direction_out, held, sems):
    sources = (solution_ref, residual_ref, direction_ref)
    outs = (solution_out, residual_out, direction_out)
    loads = [pltpu.make_async_copy(source, held.at[i], sems.at[0, i]) for i, source in enumerate(sources)]
    stores = [pltpu.make_async_copy(held.at[i], out, sems.at[1, i]) for i, out in enumerate(outs)]
    for load in loads:
        load.start()
    for load, store in zip(loads, stores):
        load.wait()
        store.start()
    for store in stores:
        store.wait()


def solution(mesh):
    panels, blks = mesh.shape["panel"], mesh.shape["blk"]

    def local(points, targets):
        rows, depth = points.shape
        cols = targets.shape[1]
        f32, bf16 = jnp.float32, jnp.bfloat16
        out = jax.ShapeDtypeStruct((cols, rows), f32)
        vmem = pl.BlockSpec(memory_space=pltpu.VMEM)
        small = [pltpu.VMEM((panels, cols // 2, 2 * cols), f32), pltpu.VMEM((blks, cols // 2, 2 * cols), f32)]
        panel_sems = pltpu.SemaphoreType.DMA((2, panels))
        blk_sems = pltpu.SemaphoreType.DMA((2, blks))
        outs = pl.pallas_call(
            functools.partial(kernel, panels, blks),
            out_shape=(out, out, out),
            in_specs=[pl.BlockSpec(memory_space=pl.ANY)] * 2,
            out_specs=(vmem, vmem, vmem),
            scratch_shapes=[
                pltpu.VMEM((panels, rows, depth), bf16),
                pltpu.VMEM((blks, rows, depth), bf16),
                pltpu.VMEM((blks, cols, rows), bf16),
                pltpu.VMEM((panels, cols, rows), f32),
                pltpu.VMEM((panels, cols, rows), f32),
                pltpu.VMEM((panels, cols, rows), f32),
                *small,
                *small,
                *small,
                panel_sems,
                blk_sems,
                blk_sems,
                panel_sems,
                panel_sems,
                panel_sems,
                blk_sems,
                panel_sems,
                blk_sems,
                panel_sems,
                blk_sems,
                pltpu.SemaphoreType.DMA((2,)),
            ],
            compiler_params=pltpu.CompilerParams(collective_id=0, has_side_effects=True),
        )(points, targets.T)
        done = pl.pallas_call(
            write,
            out_shape=(out, out, out),
            in_specs=[pl.BlockSpec(memory_space=pl.ANY)] * 3,
            out_specs=(pl.BlockSpec(memory_space=pl.ANY),) * 3,
            scratch_shapes=[pltpu.VMEM((3, cols, rows), f32), pltpu.SemaphoreType.DMA((2, 3))],
        )(*outs)
        return tuple(value.T for value in done)

    placed = P(("groups", "blk", "panel"), None)
    return jax.shard_map(
        local,
        mesh=mesh,
        in_specs=(placed, placed),
        out_specs=(placed, placed, placed),
        check_vma=False,
    )
```
